32 devices in a mesh: grp: 4 (over y, core), blk: 8 (over z, x).
Axes of the slice: x: 2, y: 2, z: 4, core: 2. Of those that a mesh axis runs over, the one named last changes fastest.
Arguments:
- pooled: bfloat16 [8192, 1536], P(('grp', 'blk')), may hold values from -6 to 6
- img_weight: bfloat16 [1536, 1152], P(('grp', 'blk')), may hold values from -0.0048828125 to 0.0048828125
- img_label: int32 [8192], P(('grp', 'blk')), may hold values from 0 to 255, as said below
- text_raw: bfloat16 [256, 1152], P('blk'), may hold values from -0.19921875 to 0.19921875
Outputs:
- grad_weight: float32 [1536, 1152], P(('grp', 'blk'))
- grad_text: float32 [256, 1152], P('blk')
The draws below stay inside these ranges and needn't reach their ends.
Inputs may be any that keep to these rules, and one draw needn't show every extreme that they name: `img_label`: every text sample is the positive of exactly 32 images.
All inputs are finite; a program needn't handle non-finite values.
Results may differ from the reference program's by a relative error of at most 0.0049.
Values may be sent and summed in bfloat16 or wider, within the bound.
No kernel may reach another device: no remote copies, remote signals or barrier semaphores. Data moves between devices by JAX's collectives and lax.ppermute only.
A program may use at most 64 MiB of HBM per device.

```python
import math
import jax
import jax.numpy as jnp
from jax import lax

DI = 1536
E = 1152
TXT_DEV = 32
IMG = 8192
TXT = 256


def draw_img_label(key, part):
    key = jax.random.fold_in(key, 7)
    order = jax.random.permutation(key, IMG)
    return (order % TXT).astype(jnp.int32)


def block_levels(stream_key, dims, pieces, low, largest):
    def one(position, parts):
        steps = jax.random.uniform(jax.random.fold_in(jax.random.fold_in(stream_key, 6), position), (parts,), jnp.float32, low / len(pieces), largest / len(pieces))
        return jnp.repeat(jnp.exp(steps), dims[position] // parts).reshape((-1,) + (1,) * (len(dims) - position - 1))

    factor_of = one(*pieces[0])
    for cut in pieces[1:]:
        factor_of = factor_of * one(*cut)
    return factor_of


def normal_values(own_key, shape, width, limit, cuts=(), kind=jnp.bfloat16):
    loudness = block_levels(own_key, shape, cuts, -0.22, 0.18) if cuts else 1.0
    drawn = jax.random.normal(own_key, shape, jnp.float32) * width * loudness
    return jnp.minimum(jnp.maximum(drawn, -limit), limit).astype(kind)


def setup_inputs(seed: int = 0) -> dict:
    streams_of = jax.random.split(jax.random.key(seed), 5)
    pooled = normal_values(streams_of[0], (IMG, DI), 1.0, 6.0, ((0, 32),))
    img_weight = normal_values(streams_of[1], (DI, E), (DI * E) ** -0.5, 0.0048828125, ((0, 32),))
    img_label = draw_img_label(jax.random.fold_in(streams_of[4], 71), 0)
    text_raw = normal_values(streams_of[3], (TXT, E), 0.03, 0.19921875, ((0, 8),))
    return dict(pooled=pooled, img_weight=img_weight, img_label=img_label, text_raw=text_raw)


epsilon = 1e-06
logit_scale = 10.0
logit_bias = -5.0

def unit_rows(raw_rows):
    inverse = lax.rsqrt(lax.optimization_barrier(jnp.sum(raw_rows * raw_rows, axis=1, keepdims=True)) + epsilon)
    return (raw_rows * inverse, inverse)

def reference(pooled, img_weight, img_label, text_raw):
    text_float, text_inverse = unit_rows(text_raw.astype(jnp.float32))
    text_unit = text_float.astype(jnp.bfloat16)
    columns = jnp.arange(TXT, dtype=jnp.int32)
    block_rows = math.gcd(IMG, 4096)
    blocks = IMG // block_rows

    def one_block(carried, inputs):
        image_rows, labels = inputs
        projected = jnp.dot(image_rows, img_weight, preferred_element_type=jnp.float32)
        embed_float, inverse = unit_rows(projected)
        embedded = embed_float.astype(jnp.bfloat16)
        logits = logit_scale * jnp.dot(embedded, text_unit.T, preferred_element_type=jnp.float32) + logit_bias
        polarity = jnp.where(labels[:, None] == columns[None, :], 1.0, -1.0).astype(jnp.float32)
        pair_slope = (-polarity * jax.nn.sigmoid(-polarity * logits) * (logit_scale / TXT_DEV)).astype(jnp.bfloat16)
        grad_embed = jnp.dot(pair_slope, text_unit, preferred_element_type=jnp.float32)
        grad_unit = jnp.dot(pair_slope.T, embedded, preferred_element_type=jnp.float32)
        grad_proj = inverse * (grad_embed - embed_float * lax.optimization_barrier(jnp.sum(grad_embed * embed_float, axis=1, keepdims=True)))
        grad_weight = jnp.dot(image_rows.T, grad_proj.astype(jnp.bfloat16), preferred_element_type=jnp.float32)
        return ((carried[0] + grad_weight, carried[1] + grad_unit), None)
    start_values = (jnp.zeros((DI, E), jnp.float32), jnp.zeros((TXT, E), jnp.float32))
    totals, _ = lax.scan(one_block, start_values, (pooled.reshape(blocks, block_rows, DI), img_label.reshape(blocks, block_rows)))
    grad_unit = totals[1]
    grad_text = text_inverse * (grad_unit - text_float * lax.optimization_barrier(jnp.sum(grad_unit * text_float, axis=1, keepdims=True)))
    return (totals[0], grad_text)
```

```python
import jax
import jax.numpy as jnp
from jax import lax
from jax.sharding import PartitionSpec as P

epsilon = 1e-06
logit_scale = 10.0
logit_bias = -5.0
axes = ("grp", "blk")


def unit_rows(raw_rows):
    inverse = lax.rsqrt(jnp.sum(raw_rows * raw_rows, axis=1, keepdims=True) + epsilon)
    return (raw_rows * inverse, inverse)


def make_shards(grp_size, blk_size):
    devices = grp_size * blk_size
    core_mask, y_mask, x_mask = blk_size, 2 * blk_size, 1
    depth = blk_size // 2
    y_size = grp_size // 2
    assert grp_size == 4 and blk_size & (blk_size - 1) == 0 and blk_size >= 2

    def swap(array, mask):
        return lax.ppermute(array, axes, [(i, i ^ mask) for i in range(devices)])

    def shards(pooled, img_weight, img_label, text_raw):
        images, width = pooled.shape
        rows, embed = img_weight.shape
        texts = text_raw.shape[0]
        half = texts // 2
        grp, blk = lax.axis_index("grp"), lax.axis_index("blk")
        core = grp % 2
        place = grp * blk_size + blk

        text_float, text_inverse = unit_rows(text_raw.astype(jnp.float32))
        text_unit = text_float.astype(jnp.bfloat16)
        own_half = lax.dynamic_slice_in_dim(text_unit, core * half, half, 0)

        own = jnp.concatenate([img_weight, own_half], axis=0)
        by_z = [own] + [None] * (depth - 1)
        for kz in range(depth - 1, 0, -1):
            by_z[kz] = swap(own, 2 * kz)
        quads, text_pairs = [], []
        for kz in range(depth):
            block = by_z[kz][:rows]
            if kz % 2 == 0:
                other = swap(by_z[kz], x_mask)
                text_other = other[rows:]
                pair = jnp.concatenate([block, other[:rows]], axis=0)
                far = swap(pair, y_mask)
                quad = jnp.concatenate([pair, far], axis=0)
            else:
                other = swap(block, y_mask)
                pair = jnp.concatenate([block, other, by_z[kz][rows:]], axis=0)
                far = swap(pair, x_mask)
                text_other = far[2 * rows :]
                quad = jnp.concatenate([block, far[:rows], other, far[rows : 2 * rows]], axis=0)
            quads.append(quad)
            text_pairs.append(jnp.concatenate([by_z[kz][rows:], text_other], axis=0))
        gathered = [jnp.concatenate([q, swap(q, core_mask)], axis=0) for q in quads]
        text_mine = jnp.concatenate(text_pairs, axis=0)
        text_all = jnp.concatenate([text_mine, swap(text_mine, core_mask)], axis=0)

        order = jnp.asarray(
            [
                ky * y_mask + kc * core_mask + kz * 2 + kx
                for kz in range(depth)
                for kc in range(2)
                for ky in range(y_size)
                for kx in range(2)
            ],
            dtype=jnp.int32,
        )
        columns = jnp.take(pooled.T.reshape(devices, rows, images), place ^ order, axis=0)
        quad_rows = 2 * y_size * rows
        columns = columns.reshape(depth, 2, quad_rows, images)
        mine = columns[:, 0].reshape(depth * quad_rows, images)
        theirs = swap(columns[:, 1].reshape(depth * quad_rows, images), core_mask)

        projected = sum(
            lax.dot_general(
                columns[kz].reshape(2 * quad_rows, images),
                gathered[kz],
                (((0,), (0,)), ((), ())),
                preferred_element_type=jnp.float32,
            )
            for kz in range(depth)
        )
        embed_float, inverse = unit_rows(projected)
        embedded = embed_float.astype(jnp.bfloat16)

        text_place = blk ^ jnp.arange(blk_size, dtype=jnp.int32)
        halves = core ^ jnp.arange(2, dtype=jnp.int32)
        text_ids = (
            text_place[None, :, None] * texts
            + halves[:, None, None] * half
            + jnp.arange(half, dtype=jnp.int32)[None, None, :]
        ).reshape(-1)
        logits = (
            logit_scale
            * lax.dot_general(
                embedded, text_all, (((1,), (1,)), ((), ())), preferred_element_type=jnp.float32
            )
            + logit_bias
        )
        polarity = jnp.where(img_label[:, None] == text_ids[None, :], 1.0, -1.0).astype(jnp.float32)
        pair_slope = (
            -polarity * jax.nn.sigmoid(-polarity * logits) * (logit_scale / texts)
        ).astype(jnp.bfloat16)
        grad_embed = jnp.dot(pair_slope, text_all, preferred_element_type=jnp.float32)
        grad_unit = lax.dot_general(
            pair_slope, embedded, (((0,), (0,)), ((), ())), preferred_element_type=jnp.float32
        )
        grad_proj = (
            inverse
            * (grad_embed - embed_float * jnp.sum(grad_embed * embed_float, axis=1, keepdims=True))
        ).astype(jnp.bfloat16)

        class_rows = blk_size * half
        grad_unit = grad_unit[:class_rows] + swap(
            grad_unit[class_rows:].astype(jnp.bfloat16), core_mask
        ).astype(jnp.float32)
        grad_unit = grad_unit.reshape(depth, 2, half, embed)
        grad_unit = grad_unit[:, 0] + swap(
            grad_unit[:, 1].astype(jnp.bfloat16), x_mask
        ).astype(jnp.float32)
        grad_unit = grad_unit + swap(grad_unit.astype(jnp.bfloat16), y_mask).astype(jnp.float32)

        grad_both = jnp.concatenate([grad_proj, swap(grad_proj, core_mask)], axis=0)
        both = jnp.concatenate([mine, theirs], axis=1).reshape(
            depth, quad_rows, 2 * images
        )
        total = None
        for kz in list(range(2, depth)) + list(range(min(2, depth))):
            part = jnp.dot(both[kz], grad_both, preferred_element_type=jnp.float32)
            part = part.reshape(y_size, 2, rows, embed)
            if kz % 2 == 0:
                part = part[0] + swap(part[1].astype(jnp.bfloat16), y_mask).astype(jnp.float32)
                part = part[0] + swap(part[1].astype(jnp.bfloat16), x_mask).astype(jnp.float32)
            else:
                part = part[:, 0] + swap(part[:, 1].astype(jnp.bfloat16), x_mask).astype(jnp.float32)
                part = part[0] + swap(part[1].astype(jnp.bfloat16), y_mask).astype(jnp.float32)
            part = jnp.concatenate([part, grad_unit[kz]], axis=0)
            if kz:
                part = swap(part.astype(jnp.bfloat16), 2 * kz).astype(jnp.float32)
            total = part if total is None else total + part
        grad_weight = total[:rows]
        half_mine = total[rows:]
        half_theirs = swap(half_mine, core_mask)
        grad_unit = jnp.where(
            core == 0,
            jnp.concatenate([half_mine, half_theirs], axis=0),
            jnp.concatenate([half_theirs, half_mine], axis=0),
        )
        grad_text = text_inverse * (
            grad_unit - text_float * jnp.sum(grad_unit * text_float, axis=1, keepdims=True)
        )
        return (grad_weight, grad_text)

    return shards


def solution(mesh):
    return jax.shard_map(
        make_shards(mesh.shape["grp"], mesh.shape["blk"]),
        mesh=mesh,
        in_specs=(
            P(("grp", "blk"), None),
            P(("grp", "blk"), None),
            P(("grp", "blk")),
            P("blk", None),
        ),
        out_specs=(P(("grp", "blk"), None), P("blk", None)),
        check_vma=False,
    )
```

```python
import jax
import jax.numpy as jnp
from jax import lax
from jax.sharding import PartitionSpec as P

epsilon = 1e-06
logit_scale = 10.0
logit_bias = -5.0
axes = ("grp", "blk")


def unit_rows(raw_rows):
    inverse = lax.rsqrt(jnp.sum(raw_rows * raw_rows, axis=1, keepdims=True) + epsilon)
    return (raw_rows * inverse, inverse)


def make_shards(grp_size, blk_size):
    devices = grp_size * blk_size
    core_mask, y_mask, x_mask = blk_size, 2 * blk_size, 1
    depth = blk_size // 2
    assert grp_size == 4 and blk_size & (blk_size - 1) == 0 and depth >= 4
    chunks = [[0], list(range(1, depth - 1)), [depth - 1]]

    def swap(array, mask):
        return lax.ppermute(array, axes, [(i, i ^ mask) for i in range(devices)])

    def swap_by_core(array, masks):
        pairs = [(i, i ^ masks[1 if i & core_mask else 0]) for i in range(devices)]
        return lax.ppermute(array, axes, pairs)

    def first(array):
        return swap_by_core(array, (x_mask, y_mask))

    def second(array):
        return swap_by_core(array, (y_mask, x_mask))

    def shards(pooled, img_weight, img_label, text_raw):
        images, width = pooled.shape
        rows, embed = img_weight.shape
        texts = text_raw.shape[0]
        quarter = texts // grp_size
        grp, blk = lax.axis_index("grp"), lax.axis_index("blk")
        core, side = grp % 2, grp // 2
        place = grp * blk_size + blk

        first_mask = jnp.where(core == 0, x_mask, y_mask)
        second_mask = jnp.where(core == 0, y_mask, x_mask)
        chunk_masks = []
        for chunk in chunks:
            kz = jnp.asarray([2 * k for k in chunk], dtype=jnp.int32)
            by_core = []
            for kc in range(2):
                f, s = (first_mask, second_mask) if kc == 0 else (second_mask, first_mask)
                j = jnp.stack([0 * f, f, s, f ^ s]).astype(jnp.int32)
                by_core.append((j[:, None] ^ kz[None, :] ^ (kc * core_mask)).reshape(-1))
            chunk_masks.append(jnp.concatenate(by_core))
        sources = [place ^ m for m in chunk_masks]

        own = jnp.concatenate(
            [img_weight, lax.dynamic_slice_in_dim(text_raw, grp * quarter, quarter, 0)], axis=0
        )[None]
        by_z = [own] + [None] * (depth - 1)
        for kz in range(1, depth):
            by_z[kz] = swap(own, 2 * kz)
        gathered = []
        last = None
        for chunk in chunks:
            block = jnp.concatenate([by_z[kz] for kz in chunk], axis=0)
            if last is not None and chunk is chunks[-1]:
                block, _ = lax.optimization_barrier((block, gathered[0]))
            pair = jnp.concatenate([block, first(block)], axis=0)
            quad = jnp.concatenate([pair, second(pair)], axis=0)
            last = quad
            gathered.append(jnp.concatenate([quad, swap(quad, core_mask)], axis=0))

        turned = pooled.T.reshape(devices, rows, images)
        columns = [jnp.take(turned, s, axis=0).reshape(2, -1, images) for s in sources]
        theirs = swap(jnp.concatenate([c[1] for c in columns], axis=0), core_mask)

        text_all = jnp.concatenate([g[:, rows:].reshape(-1, embed) for g in gathered], axis=0)
        text_all = unit_rows(text_all.astype(jnp.float32))[0].astype(jnp.bfloat16)
        text_place = jnp.concatenate(sources)
        text_first = (text_place % blk_size) * texts + (text_place // blk_size) * quarter
        text_ids = (text_first[:, None] + jnp.arange(quarter, dtype=jnp.int32)[None, :]).reshape(-1)

        projected = sum(
            lax.dot_general(
                c.reshape(-1, images),
                g[:, :rows].reshape(-1, embed),
                (((0,), (0,)), ((), ())),
                preferred_element_type=jnp.float32,
            )
            for c, g in zip(columns, gathered)
        )
        embed_float, inverse = unit_rows(projected)
        embedded = embed_float.astype(jnp.bfloat16)

        logits = (
            logit_scale
            * lax.dot_general(
                embedded, text_all, (((1,), (1,)), ((), ())), preferred_element_type=jnp.float32
            )
            + logit_bias
        )
        polarity = jnp.where(img_label[:, None] == text_ids[None, :], 1.0, -1.0).astype(jnp.float32)
        pair_slope = (
            -polarity * jax.nn.sigmoid(-polarity * logits) * (logit_scale / texts)
        ).astype(jnp.bfloat16)
        grad_embed = jnp.dot(pair_slope, text_all, preferred_element_type=jnp.float32)
        grad_proj = (
            inverse
            * (grad_embed - embed_float * jnp.sum(grad_embed * embed_float, axis=1, keepdims=True))
        ).astype(jnp.bfloat16)

        grad_unit = lax.dot_general(
            pair_slope, embedded, (((0,), (0,)), ((), ())), preferred_element_type=jnp.float32
        )
        at, keep, send = 0, [], []
        for chunk in chunks:
            size = 4 * len(chunk) * quarter
            keep.append(grad_unit[at : at + size])
            send.append(grad_unit[at + size : at + 2 * size].astype(jnp.bfloat16))
            at += 2 * size
        grad_unit = jnp.concatenate(keep, axis=0) + swap(
            jnp.concatenate(send, axis=0), core_mask
        ).astype(jnp.float32)

        grad_both = jnp.concatenate([grad_proj, swap(grad_proj, core_mask)], axis=0)
        text_at = [4 * quarter * sum(len(c) for c in chunks[:i]) for i in range(len(chunks))]
        row_at = [4 * rows * sum(len(c) for c in chunks[:i]) for i in range(len(chunks))]
        total = None
        for i in (2, 1, 0):
            chunk = chunks[i]
            count = len(chunk)
            both = jnp.concatenate(
                [columns[i][0], theirs[row_at[i] : row_at[i] + 4 * count * rows]], axis=1
            )
            part = jnp.dot(both, grad_both, preferred_element_type=jnp.float32)
            text_part = grad_unit[text_at[i] : text_at[i] + 4 * count * quarter]
            part = jnp.concatenate(
                [
                    part.reshape(4, count, rows, embed),
                    text_part.reshape(4, count, quarter, embed),
                ],
                axis=2,
            )
            part = part[:2] + second(part[2:].astype(jnp.bfloat16)).astype(jnp.float32)
            part = part[0] + first(part[1].astype(jnp.bfloat16)).astype(jnp.float32)
            for k, kz in enumerate(chunk):
                piece = part[k]
                if kz:
                    piece = swap(piece.astype(jnp.bfloat16), 2 * kz).astype(jnp.float32)
                total = piece if total is None else total + piece
        grad_weight = total[:rows]

        def joined(array, mask, position):
            other = swap(array, mask)
            return jnp.where(
                position == 0,
                jnp.concatenate([array, other], axis=0),
                jnp.concatenate([other, array], axis=0),
            )

        grad_unit = joined(joined(total[rows:], core_mask, core), y_mask, side)
        text_float, text_inverse = unit_rows(text_raw.astype(jnp.float32))
        grad_text = text_inverse * (
            grad_unit - text_float * jnp.sum(grad_unit * text_float, axis=1, keepdims=True)
        )
        return (grad_weight, grad_text)

    return shards


def solution(mesh):
    return jax.shard_map(
        make_shards(mesh.shape["grp"], mesh.shape["blk"]),
        mesh=mesh,
        in_specs=(
            P(("grp", "blk"), None),
            P(("grp", "blk"), None),
            P(("grp", "blk")),
            P("blk", None),
        ),
        out_specs=(P(("grp", "blk"), None), P("blk", None)),
        check_vma=False,
    )
```

```python
import jax
import jax.numpy as jnp
from jax import lax
from jax.sharding import PartitionSpec as P

epsilon = 1e-06
logit_scale = 10.0
logit_bias = -5.0
axes = ("grp", "blk")


def unit_rows(raw_rows):
    inverse = lax.rsqrt(jnp.sum(raw_rows * raw_rows, axis=1, keepdims=True) + epsilon)
    return (raw_rows * inverse, inverse)


def make_shards(grp_size, blk_size):
    devices = grp_size * blk_size
    core_mask, y_mask, x_mask = blk_size, 2 * blk_size, 1
    depth = blk_size // 2
    assert grp_size == 4 and blk_size & (blk_size - 1) == 0 and depth >= 4
    chunks = [[0], list(range(1, depth - 1)), [depth - 1]]

    def swap(array, mask):
        return lax.ppermute(array, axes, [(i, i ^ mask) for i in range(devices)])

    def swap_by_core(array, masks):
        pairs = [(i, i ^ masks[1 if i & core_mask else 0]) for i in range(devices)]
        return lax.ppermute(array, axes, pairs)

    def first(array):
        return swap_by_core(array, (x_mask, y_mask))

    def second(array):
        return swap_by_core(array, (y_mask, x_mask))

    def shards(pooled, img_weight, img_label, text_raw):
        images, width = pooled.shape
        rows, embed = img_weight.shape
        texts = text_raw.shape[0]
        quarter = texts // grp_size
        grp, blk = lax.axis_index("grp"), lax.axis_index("blk")
        core, side = grp % 2, grp // 2
        place = grp * blk_size + blk

        first_mask = jnp.where(core == 0, x_mask, y_mask)
        second_mask = jnp.where(core == 0, y_mask, x_mask)
        chunk_masks = []
        for chunk in chunks:
            kz = jnp.asarray([2 * k for k in chunk], dtype=jnp.int32)
            by_core = []
            for kc in range(2):
                f, s = (first_mask, second_mask) if kc == 0 else (second_mask, first_mask)
                j = jnp.stack([0 * f, f, s, f ^ s]).astype(jnp.int32)
                by_core.append((j[:, None] ^ kz[None, :] ^ (kc * core_mask)).reshape(-1))
            chunk_masks.append(jnp.concatenate(by_core))
        sources = [place ^ m for m in chunk_masks]

        own = jnp.concatenate(
            [img_weight, lax.dynamic_slice_in_dim(text_raw, grp * quarter, quarter, 0)], axis=0
        )[None]
        by_z = [own] + [None] * (depth - 1)
        for kz in range(1, depth):
            by_z[kz] = swap(by_z[kz - 1], 2) if kz % 2 and kz > 1 else swap(own, 2 * kz)
        gathered = []
        firsts, seconds = [], []
        for i, chunk in enumerate(chunks):
            block = jnp.concatenate([by_z[kz] for kz in chunk], axis=0)
            firsts.append(first(block))
            pair = jnp.concatenate([block, firsts[i]], axis=0)
            seconds.append(second(pair))
            quad = jnp.concatenate([pair, seconds[i]], axis=0)
            gathered.append(jnp.concatenate([quad, swap(quad, core_mask)], axis=0))

        turned = pooled.T.reshape(devices, rows, images)
        columns = [jnp.take(turned, s, axis=0).reshape(2, -1, images) for s in sources]
        theirs = swap(jnp.concatenate([c[1] for c in columns], axis=0), core_mask)

        text_all = jnp.concatenate([g[:, rows:].reshape(-1, embed) for g in gathered], axis=0)
        text_all = unit_rows(text_all.astype(jnp.float32))[0].astype(jnp.bfloat16)
        text_place = jnp.concatenate(sources)
        text_first = (text_place % blk_size) * texts + (text_place // blk_size) * quarter
        text_ids = (text_first[:, None] + jnp.arange(quarter, dtype=jnp.int32)[None, :]).reshape(-1)

        projected = sum(
            lax.dot_general(
                c.reshape(-1, images),
                g[:, :rows].reshape(-1, embed),
                (((0,), (0,)), ((), ())),
                preferred_element_type=jnp.float32,
            )
            for c, g in zip(columns, gathered)
        )
        embed_float, inverse = unit_rows(projected)
        embedded = embed_float.astype(jnp.bfloat16)

        logits = (
            logit_scale
            * lax.dot_general(
                embedded, text_all, (((1,), (1,)), ((), ())), preferred_element_type=jnp.float32
            )
            + logit_bias
        )
        polarity = jnp.where(img_label[:, None] == text_ids[None, :], 1.0, -1.0).astype(jnp.float32)
        pair_slope = (
            -polarity * jax.nn.sigmoid(-polarity * logits) * (logit_scale / texts)
        ).astype(jnp.bfloat16)
        grad_embed = jnp.dot(pair_slope, text_all, preferred_element_type=jnp.float32)
        grad_proj = (
            inverse
            * (grad_embed - embed_float * jnp.sum(grad_embed * embed_float, axis=1, keepdims=True))
        ).astype(jnp.bfloat16)

        grad_unit = lax.dot_general(
            pair_slope, embedded, (((0,), (0,)), ((), ())), preferred_element_type=jnp.float32
        )
        at, keep, send = 0, [], []
        for chunk in chunks:
            size = 4 * len(chunk) * quarter
            keep.append(grad_unit[at : at + size])
            send.append(grad_unit[at + size : at + 2 * size].astype(jnp.bfloat16))
            at += 2 * size
        grad_unit = jnp.concatenate(keep, axis=0) + swap(
            jnp.concatenate(send, axis=0), core_mask
        ).astype(jnp.float32)

        grad_both = jnp.concatenate([grad_proj, swap(grad_proj, core_mask)], axis=0)
        text_at = [4 * quarter * sum(len(c) for c in chunks[:i]) for i in range(len(chunks))]
        row_at = [4 * rows * sum(len(c) for c in chunks[:i]) for i in range(len(chunks))]
        total = None
        keeps, keepf, pieces = {}, {}, {}
        for i in (2, 1, 0):
            chunk = chunks[i]
            count = len(chunk)
            both = jnp.concatenate(
                [columns[i][0], theirs[row_at[i] : row_at[i] + 4 * count * rows]], axis=1
            )
            part = jnp.dot(both, grad_both, preferred_element_type=jnp.float32)
            text_part = grad_unit[text_at[i] : text_at[i] + 4 * count * quarter]
            part = jnp.concatenate(
                [
                    part.reshape(4, count, rows, embed),
                    text_part.reshape(4, count, quarter, embed),
                ],
                axis=2,
            )
            away = part[2:].astype(jnp.bfloat16)
            keeps[i] = second(away)
            part = part[:2] + keeps[i].astype(jnp.float32)
            keepf[i] = first(part[1].astype(jnp.bfloat16))
            part = part[0] + keepf[i].astype(jnp.float32)
            for k, kz in enumerate(chunk):
                pieces[kz] = part[k]
        for kz in range(3, depth, 2):
            pieces[kz - 1] += swap(pieces[kz].astype(jnp.bfloat16), 2).astype(jnp.float32)
        total = pieces[0]
        for kz in [1] + list(range(2, depth, 2)):
            total += swap(pieces[kz].astype(jnp.bfloat16), 2 * kz).astype(jnp.float32)
        grad_weight = total[:rows]

        def joined(array, mask, position):
            other = swap(array, mask)
            return jnp.where(
                position == 0,
                jnp.concatenate([array, other], axis=0),
                jnp.concatenate([other, array], axis=0),
            )

        grad_unit = joined(joined(total[rows:], core_mask, core), y_mask, side)
        text_float, text_inverse = unit_rows(text_raw.astype(jnp.float32))
        grad_text = text_inverse * (
            grad_unit - text_float * jnp.sum(grad_unit * text_float, axis=1, keepdims=True)
        )
        return (grad_weight, grad_text)

    return shards


def solution(mesh):
    return jax.shard_map(
        make_shards(mesh.shape["grp"], mesh.shape["blk"]),
        mesh=mesh,
        in_specs=(
            P(("grp", "blk"), None),
            P(("grp", "blk"), None),
            P(("grp", "blk")),
            P("blk", None),
        ),
        out_specs=(P(("grp", "blk"), None), P("blk", None)),
        check_vma=False,
    )
```

```python
import jax
import jax.numpy as jnp
from jax import lax
from jax.sharding import PartitionSpec as P

epsilon = 1e-06
logit_scale = 10.0
logit_bias = -5.0
axes = ("grp", "blk")
F32, BF16 = jnp.float32, jnp.bfloat16


def after(array, earlier):
    return lax.optimization_barrier((array, earlier))[0]


def unit_rows(raw_rows):
    inverse = lax.rsqrt(jnp.sum(raw_rows * raw_rows, axis=1, keepdims=True) + epsilon)
    return (raw_rows * inverse, inverse)


def make_shards(grp_size, blk_size):
    devices = grp_size * blk_size
    core_mask, y_mask, x_mask = blk_size, 2 * blk_size, 1
    depth = blk_size // 2
    assert grp_size == 4 and blk_size & (blk_size - 1) == 0 and depth >= 4

    def swap(array, mask):
        return lax.ppermute(array, axes, [(i, i ^ mask) for i in range(devices)])

    def swap_by_core(array, masks):
        pairs = [(i, i ^ masks[1 if i & core_mask else 0]) for i in range(devices)]
        return lax.ppermute(array, axes, pairs)

    def first(array):
        return swap_by_core(array, (x_mask, y_mask))

    def second(array):
        return swap_by_core(array, (y_mask, x_mask))

    def shards(pooled, img_weight, img_label, text_raw):
        images, width = pooled.shape
        rows, embed = img_weight.shape
        texts = text_raw.shape[0]
        quarter = texts // grp_size
        grp, blk = lax.axis_index("grp"), lax.axis_index("blk")
        core, side = grp % 2, grp // 2
        place = grp * blk_size + blk

        own = jnp.concatenate(
            [img_weight, lax.dynamic_slice_in_dim(text_raw, grp * quarter, quarter, 0)], axis=0
        )[None]
        by_z = [own]
        for kz in range(1, depth):
            by_z.append(swap(by_z[kz - 1], 2) if kz % 2 and kz > 1 else swap(own, 2 * kz))
        quads, firsts = [], []
        for kz, block in enumerate(by_z):
            if kz == 1:
                block = after(block, firsts[0])
            if kz == 2:
                block = after(block, by_z[1])
            firsts.append(first(block))
            pair = jnp.concatenate([by_z[kz], firsts[kz]], axis=0)
            quads.append(jnp.concatenate([pair, second(pair)], axis=0))
        gathered = [
            jnp.concatenate(quads, axis=0),
            jnp.concatenate([swap(quad, core_mask) for quad in quads], axis=0),
        ]

        def block_sources(kc):
            f = jnp.where((core ^ kc) == 0, x_mask, y_mask)
            s = x_mask + y_mask - f
            number = jnp.arange(4 * depth, dtype=jnp.int32)
            j, kz = number % 4, number // 4
            return place ^ (kc * core_mask) ^ (2 * kz) ^ ((j % 2) * f) ^ ((j // 2) * s)

        sources = jnp.concatenate([block_sources(0), block_sources(1)])

        turned = pooled.T.reshape(devices, rows, images)
        columns = jnp.take(turned, sources, axis=0).reshape(2, -1, images)
        mine, other = columns[0], columns[1]
        theirs = swap(other, core_mask)

        text_all = jnp.concatenate([g[:, rows:].reshape(-1, embed) for g in gathered], axis=0)
        text_all = unit_rows(text_all.astype(F32))[0].astype(BF16)
        text_first = (sources % blk_size) * texts + (sources // blk_size) * quarter
        text_ids = (text_first[:, None] + jnp.arange(quarter, dtype=jnp.int32)[None, :]).reshape(-1)

        def partly(column, found):
            return lax.dot_general(
                column,
                found[:, :rows].reshape(-1, embed),
                (((0,), (0,)), ((), ())),
                preferred_element_type=F32,
            )

        projected = partly(mine, gathered[0]) + partly(other, gathered[1])
        embed_float, inverse = unit_rows(projected)
        embedded = embed_float.astype(BF16)
        embedded_theirs = swap(embedded, core_mask)

        logits = (
            logit_scale
            * lax.dot_general(embedded, text_all, (((1,), (1,)), ((), ())), preferred_element_type=F32)
            + logit_bias
        )
        polarity = jnp.where(img_label[:, None] == text_ids[None, :], 1.0, -1.0).astype(F32)
        pair_slope = (
            -polarity * jax.nn.sigmoid(-polarity * logits) * (logit_scale / texts)
        ).astype(BF16)
        half = pair_slope.shape[1] // 2
        slope_theirs = swap(pair_slope[:, half:], core_mask)
        grad_embed = jnp.dot(pair_slope, text_all, preferred_element_type=F32)
        grad_proj = (
            inverse
            * (grad_embed - embed_float * jnp.sum(grad_embed * embed_float, axis=1, keepdims=True))
        ).astype(BF16)
        proj_theirs = swap(grad_proj, core_mask)

        across = (((0,), (0,)), ((), ()))
        grad_unit = lax.dot_general(
            pair_slope[:, :half], embedded, across, preferred_element_type=F32
        ) + lax.dot_general(slope_theirs, embedded_theirs, across, preferred_element_type=F32)
        grad_unit = grad_unit.reshape(depth, 4, quarter, embed)
        mine = mine.reshape(depth, 4 * rows, images)
        theirs = theirs.reshape(depth, 4 * rows, images)

        def send(array):
            return array.astype(BF16)

        halves, pieces = {}, {}
        for kz in range(depth - 1, -1, -1):
            part = jnp.dot(mine[kz], grad_proj, preferred_element_type=F32)
            part += jnp.dot(theirs[kz], proj_theirs, preferred_element_type=F32)
            part = jnp.concatenate([part.reshape(4, rows, embed), grad_unit[kz]], axis=1)
            away = send(part[2:])
            if kz + 2 in halves:
                away = after(away, halves[kz + 2])
            halves[kz] = second(away)
            part = part[:2] + halves[kz].astype(F32)
            pieces[kz] = part[0] + first(send(part[1])).astype(F32)
        for kz in range(3, depth, 2):
            pieces[kz - 1] += swap(send(pieces[kz]), 2).astype(F32)
        total = pieces[0]
        for kz in [1] + list(range(2, depth, 2)):
            total += swap(send(pieces[kz]), 2 * kz).astype(F32)
        grad_weight, grad_unit = total[:rows], total[rows:]

        def joined(array, mask, position):
            other = swap(array, mask)
            return jnp.where(
                position == 0,
                jnp.concatenate([array, other], axis=0),
                jnp.concatenate([other, array], axis=0),
            )

        grad_unit = joined(joined(grad_unit, core_mask, core), y_mask, side)
        text_float, text_inverse = unit_rows(text_raw.astype(F32))
        grad_text = text_inverse * (
            grad_unit - text_float * jnp.sum(grad_unit * text_float, axis=1, keepdims=True)
        )
        return (grad_weight, grad_text)

    return shards


def solution(mesh):
    return jax.shard_map(
        make_shards(mesh.shape["grp"], mesh.shape["blk"]),
        mesh=mesh,
        in_specs=(
            P(("grp", "blk"), None),
            P(("grp", "blk"), None),
            P(("grp", "blk")),
            P("blk", None),
        ),
        out_specs=(P(("grp", "blk"), None), P("blk", None)),
        check_vma=False,
    )
```

```python
import jax
import jax.numpy as jnp
from jax import lax
from jax.sharding import PartitionSpec as P

epsilon = 1e-06
logit_scale = 10.0
logit_bias = -5.0
axes = ("grp", "blk")
F32, BF16 = jnp.float32, jnp.bfloat16


def after(array, earlier):
    return lax.optimization_barrier((array, earlier))[0]


def unit_rows(raw_rows):
    inverse = lax.rsqrt(jnp.sum(raw_rows * raw_rows, axis=1, keepdims=True) + epsilon)
    return (raw_rows * inverse, inverse)


def make_shards(grp_size, blk_size):
    devices = grp_size * blk_size
    core_mask, y_mask, x_mask = blk_size, 2 * blk_size, 1
    depth = blk_size // 2
    assert grp_size == 4 and blk_size & (blk_size - 1) == 0 and depth >= 4

    def swap(array, mask):
        return lax.ppermute(array, axes, [(i, i ^ mask) for i in range(devices)])

    def swap_by_core(array, masks):
        pairs = [(i, i ^ masks[1 if i & core_mask else 0]) for i in range(devices)]
        return lax.ppermute(array, axes, pairs)

    def first(array):
        return swap_by_core(array, (x_mask, y_mask))

    def second(array):
        return swap_by_core(array, (y_mask, x_mask))

    def shards(pooled, img_weight, img_label, text_raw):
        images, width = pooled.shape
        rows, embed = img_weight.shape
        texts = text_raw.shape[0]
        quarter = texts // grp_size
        grp, blk = lax.axis_index("grp"), lax.axis_index("blk")
        core = grp % 2
        place = grp * blk_size + blk

        own = jnp.concatenate(
            [img_weight, lax.dynamic_slice_in_dim(text_raw, grp * quarter, quarter, 0)], axis=0
        )[None]
        by_z = [own]
        for kz in range(1, depth):
            by_z.append(swap(by_z[kz - 1], 2) if kz % 2 and kz > 1 else swap(own, 2 * kz))
        quads, firsts = [], []
        for kz, block in enumerate(by_z):
            if kz == 1:
                block = after(block, firsts[0])
            if kz == 2:
                block = after(block, by_z[1])
            firsts.append(first(block))
            pair = jnp.concatenate([by_z[kz], firsts[kz]], axis=0)
            quads.append(jnp.concatenate([pair, second(pair)], axis=0))
        gathered = [
            jnp.concatenate(quads, axis=0),
            jnp.concatenate([swap(quad, core_mask) for quad in quads], axis=0),
        ]

        def block_sources(kc):
            f = jnp.where((core ^ kc) == 0, x_mask, y_mask)
            s = x_mask + y_mask - f
            number = jnp.arange(4 * depth, dtype=jnp.int32)
            j, kz = number % 4, number // 4
            return place ^ (kc * core_mask) ^ (2 * kz) ^ ((j % 2) * f) ^ ((j // 2) * s)

        sources = jnp.concatenate([block_sources(0), block_sources(1)])

        turned = pooled.T.reshape(devices, rows, images)
        columns = jnp.take(turned, sources, axis=0).reshape(2, -1, images)
        mine, other = columns[0], columns[1]
        theirs = swap(other, core_mask)

        text_all = jnp.concatenate([g[:, rows:].reshape(-1, embed) for g in gathered], axis=0)
        text_all = unit_rows(text_all.astype(F32))[0].astype(BF16)
        text_first = (sources % blk_size) * texts + (sources // blk_size) * quarter
        text_ids = (text_first[:, None] + jnp.arange(quarter, dtype=jnp.int32)[None, :]).reshape(-1)

        def partly(column, found):
            return lax.dot_general(
                column,
                found[:, :rows].reshape(-1, embed),
                (((0,), (0,)), ((), ())),
                preferred_element_type=F32,
            )

        projected = partly(mine, gathered[0]) + partly(other, gathered[1])
        embed_float, inverse = unit_rows(projected)
        embedded = embed_float.astype(BF16)
        embedded_theirs = swap(embedded, core_mask)

        logits = (
            logit_scale
            * lax.dot_general(embedded, text_all, (((1,), (1,)), ((), ())), preferred_element_type=F32)
            + logit_bias
        )
        polarity = jnp.where(img_label[:, None] == text_ids[None, :], 1.0, -1.0).astype(F32)
        pair_slope = (
            -polarity * jax.nn.sigmoid(-polarity * logits) * (logit_scale / texts)
        ).astype(BF16)
        half = pair_slope.shape[1] // 2
        slope_theirs = swap(pair_slope[:, half:], core_mask)
        grad_embed = jnp.dot(pair_slope, text_all, preferred_element_type=F32)
        grad_proj = (
            inverse
            * (grad_embed - embed_float * jnp.sum(grad_embed * embed_float, axis=1, keepdims=True))
        ).astype(BF16)
        proj_theirs = swap(grad_proj, core_mask)

        across = (((0,), (0,)), ((), ()))
        grad_unit = lax.dot_general(
            pair_slope[:, :half], embedded, across, preferred_element_type=F32
        ) + lax.dot_general(slope_theirs, embedded_theirs, across, preferred_element_type=F32)
        grad_unit = grad_unit.reshape(depth, 4, quarter, embed)
        mine = mine.reshape(depth, 4 * rows, images)
        theirs = theirs.reshape(depth, 4 * rows, images)

        def send(array):
            return array.astype(BF16)

        halves, pieces = {}, {}
        for kz in range(depth - 1, -1, -1):
            part = jnp.dot(mine[kz], grad_proj, preferred_element_type=F32)
            part += jnp.dot(theirs[kz], proj_theirs, preferred_element_type=F32)
            part = jnp.concatenate([part.reshape(4, rows, embed), grad_unit[kz]], axis=1)
            away = send(part[2:])
            if kz + 2 in halves:
                away = after(away, halves[kz + 2])
            halves[kz] = second(away)
            part = part[:2] + halves[kz].astype(F32)
            pieces[kz] = part[0] + first(send(part[1])).astype(F32)
        for kz in range(3, depth, 2):
            pieces[kz - 1] += swap(send(pieces[kz]), 2).astype(F32)
        total = pieces[0]
        for kz in [1] + list(range(2, depth, 2)):
            total += swap(send(pieces[kz]), 2 * kz).astype(F32)
        grad_weight, grad_unit = total[:rows], total[rows:]

        quarters = [grad_unit] + [swap(grad_unit, g * core_mask) for g in range(1, grp_size)]
        ordered = []
        for g in range(grp_size):
            found = quarters[0]
            for k in range(1, grp_size):
                found = jnp.where(grp == (g ^ k), quarters[k], found)
            ordered.append(found)
        grad_unit = jnp.concatenate(ordered, axis=0)
        text_float, text_inverse = unit_rows(text_raw.astype(F32))
        grad_text = text_inverse * (
            grad_unit - text_float * jnp.sum(grad_unit * text_float, axis=1, keepdims=True)
        )
        return (grad_weight, grad_text)

    return shards


def solution(mesh):
    return jax.shard_map(
        make_shards(mesh.shape["grp"], mesh.shape["blk"]),
        mesh=mesh,
        in_specs=(
            P(("grp", "blk"), None),
            P(("grp", "blk"), None),
            P(("grp", "blk")),
            P("blk", None),
        ),
        out_specs=(P(("grp", "blk"), None), P("blk", None)),
        check_vma=False,
    )
```

```python
import jax
import jax.numpy as jnp
from jax import lax
from jax.sharding import PartitionSpec as P

epsilon = 1e-06
logit_scale = 10.0
logit_bias = -5.0
axes = ("grp", "blk")
F32, BF16 = jnp.float32, jnp.bfloat16


def after(array, earlier):
    return lax.optimization_barrier((array, earlier))[0]


def unit_rows(raw_rows):
    inverse = lax.rsqrt(jnp.sum(raw_rows * raw_rows, axis=1, keepdims=True) + epsilon)
    return (raw_rows * inverse, inverse)


def make_shards(grp_size, blk_size):
    devices = grp_size * blk_size
    core_mask, y_mask, x_mask = blk_size, 2 * blk_size, 1
    depth = blk_size // 2
    assert grp_size == 4 and blk_size & (blk_size - 1) == 0 and depth >= 4

    def swap(array, mask):
        return lax.ppermute(array, axes, [(i, i ^ mask) for i in range(devices)])

    def swap_by_core(array, masks):
        pairs = [(i, i ^ masks[1 if i & core_mask else 0]) for i in range(devices)]
        return lax.ppermute(array, axes, pairs)

    def first(array):
        return swap_by_core(array, (x_mask, y_mask))

    def second(array):
        return swap_by_core(array, (y_mask, x_mask))

    def shards(pooled, img_weight, img_label, text_raw):
        images, width = pooled.shape
        rows, embed = img_weight.shape
        texts = text_raw.shape[0]
        quarter = texts // grp_size
        grp, blk = lax.axis_index("grp"), lax.axis_index("blk")
        core = grp % 2
        place = grp * blk_size + blk

        own = jnp.concatenate(
            [img_weight, lax.dynamic_slice_in_dim(text_raw, grp * quarter, quarter, 0)], axis=0
        )[None]
        by_z = [own]
        for kz in range(1, depth):
            by_z.append(swap(by_z[kz - 1], 2) if kz % 2 and kz > 1 else swap(own, 2 * kz))
        quads, firsts = [], []
        for kz, block in enumerate(by_z):
            if kz == 1:
                block = after(block, firsts[0])
            if kz == 2:
                block = after(block, by_z[1])
            if kz % 2 and kz > 1:
                firsts.append(swap(firsts[kz - 1], 2))
            else:
                firsts.append(first(block))
            pair = jnp.concatenate([by_z[kz], firsts[kz]], axis=0)
            quads.append(jnp.concatenate([pair, second(pair)], axis=0))
        gathered = [
            jnp.concatenate(quads, axis=0),
            jnp.concatenate([swap(quad, core_mask) for quad in quads], axis=0),
        ]

        def block_sources(kc):
            f = jnp.where((core ^ kc) == 0, x_mask, y_mask)
            s = x_mask + y_mask - f
            number = jnp.arange(4 * depth, dtype=jnp.int32)
            j, kz = number % 4, number // 4
            return place ^ (kc * core_mask) ^ (2 * kz) ^ ((j % 2) * f) ^ ((j // 2) * s)

        sources = jnp.concatenate([block_sources(0), block_sources(1)])

        turned = pooled.T.reshape(devices, rows, images)
        columns = jnp.take(turned, sources, axis=0).reshape(2, -1, images)
        mine, other = columns[0], columns[1]
        theirs = swap(after(other, firsts[2]), core_mask)

        text_all = jnp.concatenate([g[:, rows:].reshape(-1, embed) for g in gathered], axis=0)
        text_all = unit_rows(text_all.astype(F32))[0].astype(BF16)
        text_first = (sources % blk_size) * texts + (sources // blk_size) * quarter
        text_ids = (text_first[:, None] + jnp.arange(quarter, dtype=jnp.int32)[None, :]).reshape(-1)

        def partly(column, found):
            return lax.dot_general(
                column,
                found[:, :rows].reshape(-1, embed),
                (((0,), (0,)), ((), ())),
                preferred_element_type=F32,
            )

        projected = partly(mine, gathered[0]) + partly(other, gathered[1])
        embed_float, inverse = unit_rows(projected)
        embedded = embed_float.astype(BF16)
        embedded_theirs = swap(embedded, core_mask)

        logits = (
            logit_scale
            * lax.dot_general(embedded, text_all, (((1,), (1,)), ((), ())), preferred_element_type=F32)
            + logit_bias
        )
        polarity = jnp.where(img_label[:, None] == text_ids[None, :], 1.0, -1.0).astype(F32)
        pair_slope = (
            -polarity * jax.nn.sigmoid(-polarity * logits) * (logit_scale / texts)
        ).astype(BF16)
        half = pair_slope.shape[1] // 2
        slope_theirs = swap(pair_slope[:, half:], core_mask)
        grad_embed = jnp.dot(pair_slope, text_all, preferred_element_type=F32)
        grad_proj = (
            inverse
            * (grad_embed - embed_float * jnp.sum(grad_embed * embed_float, axis=1, keepdims=True))
        ).astype(BF16)
        proj_theirs = swap(grad_proj, core_mask)

        across = (((0,), (0,)), ((), ()))
        grad_unit = lax.dot_general(
            pair_slope[:, :half], embedded, across, preferred_element_type=F32
        ) + lax.dot_general(slope_theirs, embedded_theirs, across, preferred_element_type=F32)
        grad_unit = grad_unit.reshape(depth, 4, quarter, embed)
        mine = mine.reshape(depth, 4 * rows, images)
        theirs = theirs.reshape(depth, 4 * rows, images)

        def send(array):
            return array.astype(BF16)

        halves, pieces = {}, {}
        for kz in range(depth - 1, -1, -1):
            part = jnp.dot(mine[kz], grad_proj, preferred_element_type=F32)
            part += jnp.dot(theirs[kz], proj_theirs, preferred_element_type=F32)
            part = jnp.concatenate([part.reshape(4, rows, embed), grad_unit[kz]], axis=1)
            away = send(part[2:])
            if kz + 2 in halves:
                away = after(away, halves[kz + 2])
            halves[kz] = second(away)
            part = part[:2] + halves[kz].astype(F32)
            pieces[kz] = part[0] + first(send(part[1])).astype(F32)
        for kz in range(3, depth, 2):
            pieces[kz - 1] += swap(send(pieces[kz]), 2).astype(F32)
        total = pieces[0]
        for kz in [1] + list(range(2, depth, 2)):
            total += swap(send(pieces[kz]), 2 * kz).astype(F32)
        grad_weight, grad_unit = total[:rows], total[rows:]

        quarters = [grad_unit] + [swap(grad_unit, g * core_mask) for g in range(1, grp_size)]
        ordered = []
        for g in range(grp_size):
            found = quarters[0]
            for k in range(1, grp_size):
                found = jnp.where(grp == (g ^ k), quarters[k], found)
            ordered.append(found)
        grad_unit = jnp.concatenate(ordered, axis=0)
        text_float, text_inverse = unit_rows(text_raw.astype(F32))
        grad_text = text_inverse * (
            grad_unit - text_float * jnp.sum(grad_unit * text_float, axis=1, keepdims=True)
        )
        return (grad_weight, grad_text)

    return shards


def solution(mesh):
    return jax.shard_map(
        make_shards(mesh.shape["grp"], mesh.shape["blk"]),
        mesh=mesh,
        in_specs=(
            P(("grp", "blk"), None),
            P(("grp", "blk"), None),
            P(("grp", "blk")),
            P("blk", None),
        ),
        out_specs=(P(("grp", "blk"), None), P("blk", None)),
        check_vma=False,
    )
```
